512 devices in a mesh: blk: 128 (over x, z_lo, y, core), rows: 4 (over z_hi).
Axes of the slice: x: 4, y: 8, z: 8 (z_hi: 4, z_lo: 2; z = z_hi * 2 + z_lo), core: 2. Of those that a mesh axis runs over, the one named last changes fastest.
Arguments:
- weight: bfloat16 [1024, 16384], P('blk', 'rows')
- factor: bfloat16 [16384, 16384], P('rows', 'blk')
- pairing: int32 [4, 64], replicated, may hold values from 0 to 63, each once within a row
Outputs:
- rotated: float32 [1024, 16384], P('rows', 'blk')
- right_factor: float32 [16384, 16384], P('rows', 'blk')
The draws below stay inside these ranges and needn't reach their ends.
Inputs may be any that keep to these rules, and one draw needn't show every extreme that they name: Each row of pairing lists every column index of a block once.
All inputs are finite; a program needn't handle non-finite values.
Results may differ from the reference program's by a relative error of at most 0.0003.
Values may be sent and summed in bfloat16 or wider, within the bound.
A program may use at most 64 MiB of HBM per device.

```python
import math
import jax
import jax.numpy as jnp
from jax import lax

BLOCK = 64
STEPS = 4
ROWS = 1024
PAIRS = 128
COLS = 16384


def draw_weight(key, part):
    key = jax.random.fold_in(key, 11)
    noise_key, common_key, scale_key = jax.random.split(key, 3)
    noise_draw = jax.random.normal(noise_key, (ROWS, COLS), jnp.float32)
    scales = jnp.exp(jax.random.uniform(scale_key, (ROWS, 1), jnp.float32, math.log(0.3), math.log(3.0)))
    mixing = 0.6
    common = jax.random.normal(common_key, (ROWS, 1), jnp.float32)
    return (scales * (noise_draw + mixing * common) / math.sqrt(COLS)).astype(jnp.bfloat16)


def draw_factor(key, part):
    key = jax.random.fold_in(key, 23)
    noise_key, diag_key, scale_key = jax.random.split(key, 3)
    noise_draw = jax.random.normal(noise_key, (COLS, COLS), jnp.float32)
    scales = jnp.exp(jax.random.uniform(scale_key, (1, COLS), jnp.float32, math.log(0.3), math.log(3.0)))
    diagonal = jax.random.uniform(diag_key, (COLS, 1), jnp.float32, 1.0, 2.0)
    row_index = lax.broadcasted_iota(jnp.int32, (COLS, COLS), 0)
    col_index = lax.broadcasted_iota(jnp.int32, (COLS, COLS), 1)
    below = jnp.where(row_index > col_index, noise_draw, 0.0)
    on_diagonal = jnp.where(row_index == col_index, diagonal * math.sqrt(COLS), 0.0)
    return (scales * (below + on_diagonal)).astype(jnp.bfloat16)


def setup_inputs(seed: int = 0) -> dict:
    key_list = jax.random.split(jax.random.key(seed), 4)
    return {
        "weight": draw_weight(jax.random.fold_in(key_list[3], 71), 0),
        "factor": draw_factor(jax.random.fold_in(key_list[3], 71), 0),
        "pairing": jax.vmap(lambda own: jax.random.permutation(own, BLOCK))(jax.random.split(key_list[2], STEPS)).reshape((STEPS, BLOCK)).astype(jnp.int32),
    }


def turn_blocks(upper_cols, lower_cols, cosine, sine_part, pair_order, inverse):
    partner = jnp.take(lower_cols, pair_order, axis=2)
    new_upper = cosine * upper_cols + sine_part * partner
    new_partner = cosine * partner - sine_part * upper_cols
    return new_upper, jnp.take(new_partner, inverse, axis=2)


def arrange(upper_cols, lower_cols):
    offset = STEPS - 1
    stacked = jnp.stack([jnp.roll(upper_cols, offset, axis=1), jnp.roll(lower_cols, offset, axis=1)], axis=2)
    return stacked.reshape(upper_cols.shape[0], COLS)


def reference(weight, factor, pairing):
    whitened = jnp.dot(weight, factor, preferred_element_type=jnp.float32)
    blocks = whitened.reshape(ROWS, PAIRS, 2, BLOCK)
    upper_cols = blocks[:, :, 0, :]
    lower_cols = blocks[:, :, 1, :]
    history = []
    for step_index in range(STEPS):
        pair_order = pairing[step_index].astype(jnp.int32)
        inverse = jnp.argsort(pair_order).astype(jnp.int32)
        if step_index > 0:
            lower_cols = jnp.roll(lower_cols, -2, axis=1)
        partner = jnp.take(lower_cols, pair_order, axis=2)
        upper_norm = jnp.sum(upper_cols * upper_cols, axis=0)
        lower_norm = jnp.sum(partner * partner, axis=0)
        cross_term = jnp.sum(upper_cols * partner, axis=0)
        rotation_angle = 0.5 * jnp.arctan2(2.0 * cross_term, upper_norm - lower_norm)
        cosine = jnp.cos(rotation_angle)
        sine_part = jnp.sin(rotation_angle)
        history.append((cosine, sine_part, pair_order, inverse))
        upper_cols, lower_cols = turn_blocks(upper_cols, lower_cols, cosine, sine_part, pair_order, inverse)
    rotated = arrange(upper_cols, lower_cols)

    def evolve(factor_rows):
        parts = factor_rows.astype(jnp.float32).reshape(factor_rows.shape[0], PAIRS, 2, BLOCK)
        up_cols = parts[:, :, 0, :]
        low_cols = parts[:, :, 1, :]
        for step_index in range(STEPS):
            cosine, sine_part, pair_order, inverse = history[step_index]
            if step_index > 0:
                low_cols = jnp.roll(low_cols, -2, axis=1)
            up_cols, low_cols = turn_blocks(up_cols, low_cols, cosine, sine_part, pair_order, inverse)
        return arrange(up_cols, low_cols)

    right_factor = lax.map(evolve, factor.reshape(PAIRS, COLS // PAIRS, COLS)).reshape(COLS, COLS)
    return rotated, right_factor
```

```python
import functools
import jax
import jax.numpy as jnp
from jax import lax
from jax.experimental import pallas as pl
from jax.experimental.pallas import tpu as pltpu
from jax.sharding import PartitionSpec as P

MESH = pl.DeviceIdType.MESH
BLOCK = 64
STEPS = 4
NX, NZ, NY, NR = 4, 2, 8, 4
NB = 2 * NX * NZ * NY
HOPS = ((1, 0, 0), (3, 0, 0), (0, 1, 0), (0, 0, 1), (0, 0, 7))
TREE = (
    (0, 1, 0, 2), (3, 0, 0, 1), (0, 0, 1, 3), (0, 0, 7, 4), (1, 0, 0, 0), (2, 0, 0, 1), (1, 1, 0, 0), (0, 0, 6, 4),
    (0, 0, 2, 3), (0, 1, 7, 2), (1, 0, 7, 0), (3, 0, 7, 1), (0, 1, 1, 3), (3, 1, 0, 2), (3, 0, 1, 1), (1, 0, 1, 0),
    (1, 1, 7, 4), (0, 1, 6, 2), (0, 0, 3, 3), (2, 1, 0, 0), (3, 1, 7, 1), (1, 0, 6, 4), (0, 1, 2, 3), (2, 0, 7, 0),
    (3, 1, 1, 1), (1, 1, 1, 2), (1, 0, 2, 3), (3, 0, 6, 4), (3, 0, 2, 1), (2, 0, 1, 0), (0, 0, 4, 3), (0, 1, 5, 4),
    (0, 1, 3, 2), (2, 1, 7, 1), (1, 0, 3, 0), (1, 1, 6, 2), (2, 0, 6, 4), (3, 1, 2, 3), (3, 1, 6, 1), (1, 1, 2, 0),
    (2, 0, 2, 3), (3, 0, 5, 4), (2, 1, 1, 2), (3, 0, 3, 1), (1, 1, 5, 0), (0, 1, 4, 2), (2, 1, 6, 4), (3, 0, 4, 1),
    (1, 1, 3, 0), (0, 0, 5, 2), (3, 1, 3, 1), (2, 1, 2, 0), (3, 1, 5, 2), (2, 0, 3, 1), (2, 1, 5, 0), (3, 1, 4, 1),
    (1, 0, 5, 0), (2, 1, 3, 1), (1, 0, 4, 0), (2, 0, 4, 1), (1, 1, 4, 0), (2, 1, 4, 1), (2, 0, 5, 0),
)
PLANES = (0, 3, 1, 2)
LEAVES = tuple((b3, b2, b1) for b3 in (0, 1) for b2 in (0, 1) for b1 in (0, 1))


def plus(offset, hop):
    return tuple((a + b) % n for a, b, n in zip(offset, hop, (NX, NZ, NY)))


def turn(p_minus_r, q):
    y = 2.0 * q
    x = p_minus_r
    top = jnp.maximum(jnp.abs(x), jnp.abs(y))
    safe = jnp.where(top > 0.0, top, 1.0)
    xs = jnp.where(top > 0.0, x / safe, 1.0)
    ys = jnp.where(top > 0.0, y / safe, 0.0)
    h = jnp.sqrt(xs * xs + ys * ys)
    big = jnp.sqrt(0.5 * (1.0 + jnp.abs(xs) / h))
    small = jnp.abs(ys) / (2.0 * h * big)
    cosine = jnp.where(x >= 0.0, big, small)
    size = jnp.where(x >= 0.0, small, big)
    return cosine, jnp.where(y < 0.0, -size, size)


def split3(x):
    hi = x.astype(jnp.bfloat16)
    rest = x - hi.astype(jnp.float32)
    mid = rest.astype(jnp.bfloat16)
    low = (rest - mid.astype(jnp.float32)).astype(jnp.bfloat16)
    return hi, mid, low


def dot(a, b, dims=(((1,), (0,)), ((), ()))):
    return lax.dot_general(a, b, dims, preferred_element_type=jnp.float32)


def gram_plan():
    rows = {}
    for n in range(8):
        rows["pr", n] = len(rows)
        rows["q", n] = len(rows)
    for level in (1, 2, 3):
        for n in range(8):
            for m in range(8):
                if n >> level == m >> level and (n >> (level - 1)) & 1 == 0 and (m >> (level - 1)) & 1 == 1:
                    rows["same", n, m] = len(rows)
                    rows["cross", n, m] = len(rows)
    return rows


GRAM = gram_plan()


def kernel(
    w_ref, f_ref, pair_ref, rot_ref, right_ref,
    wbuf, fbuf, part, rsbuf, wsum, xbuf, ybuf, gram, gbuf, ebuf, mbuf, coef,
    wsend, wrecv, own_sem, fsend, frecv, rssend, rsrecv, xsend, xrecv, gsend, grecv,
):
    b = lax.axis_index("blk")
    r = lax.axis_index("rows")
    core = lax.rem(b, 2)
    y = lax.rem(b // 2, NY)
    z = lax.rem(b // (2 * NY), NZ)
    x = b // (2 * NY * NZ)
    sigma = 1 - 2 * core

    def blk(shift):
        return (lax.rem(b + shift + NB, NB), r)

    def hop(h):
        dx, dz, dy = HOPS[h]
        index = lax.rem(x + dx, NX) * (2 * NY * NZ) + lax.rem(z + dz, NZ) * (2 * NY) + lax.rem(y + dy, NY) * 2 + core
        return (index, r)

    def peer(shift):
        return (b, lax.rem(r + shift, NR))

    own_factor = pltpu.make_async_copy(f_ref, fbuf.at[0], own_sem)
    own_factor.start()

    barrier = pltpu.get_barrier_semaphore()
    greet = [hop(h) for h in range(5)] + [peer(s) for s in (1, 2, 3)]
    greet += [blk(sigma * s) for s in (1, -1, 3, -3, 2, -2, -4)]
    for target in greet:
        pl.semaphore_signal(barrier, inc=1, device_id=target, device_id_type=MESH)

    def remote(src, dst, send, recv, target):
        return pltpu.make_async_remote_copy(
            src_ref=src, dst_ref=dst, send_sem=send, recv_sem=recv, device_id=target, device_id_type=MESH
        )

    def slot(offset):
        return (offset[0] * NZ + offset[1]) * NY + lax.rem(y - offset[2] + NY, NY)

    index_of = {entry[:3]: k for k, entry in enumerate(TREE)}
    children = {}
    for k, entry in enumerate(TREE):
        back = tuple(-v for v in HOPS[entry[3]])
        children.setdefault(plus(entry[:3], back), []).append(k)
    pending = []

    def weight_copy(k):
        offset, h = TREE[k][:3], TREE[k][3]
        source = plus(offset, tuple(-v for v in HOPS[h]))
        line = offset[0] * NZ + offset[1]
        return remote(
            wbuf.at[slot(source)],
            wbuf.at[line * NY + lax.rem(y - source[2] + NY, NY)],
            wsend.at[k],
            wrecv.at[k],
            hop(h),
        )

    def forward(offset):
        for k in children.get(offset, ()):
            copy = weight_copy(k)
            copy.start()
            pending.append(copy)

    def arrived(k):
        weight_copy(k).wait_recv()

    wide = w_ref[...].astype(jnp.float32)
    half = wide.shape[1] // 2
    wbuf[y] = jnp.concatenate([wide[:, :half], wide[:, half:]], axis=0).astype(jnp.bfloat16)

    own_factor.wait()
    pl.semaphore_wait(barrier, len(greet))
    forward((0, 0, 0))
    swap = remote(fbuf.at[0], fbuf.at[1], fsend.at[0], frecv.at[0], blk(sigma))
    swap.start()
    pending.append(swap)

    depth = fbuf.shape[1]
    halves = [pl.ds(0, depth // 2), pl.ds(depth // 2, depth // 2)]

    def factor_out():
        for k, rows in enumerate(halves):
            for base, shift, place in ((1, -1, 2), (3, 3, 4)):
                copy = remote(
                    fbuf.at[0, rows], fbuf.at[place, rows], fsend.at[base + k], frecv.at[base + k], blk(sigma * shift)
                )
                copy.start()
                pending.append(copy)

    waited = set()
    last_parent = max(k for k, entry in enumerate(TREE) if entry[:3] in children)
    for k in range(last_parent + 1):
        if TREE[k][:3] in children:
            arrived(k)
            waited.add(k)
            forward(TREE[k][:3])
        if k == 30:
            factor_out()

    swap.wait_recv()
    kdim = half
    lines = []

    def whiten(line):
        dx, dz = line // NZ, line % NZ
        for dy in range(NY):
            if (dx, dz, dy) != (0, 0, 0) and index_of[dx, dz, dy] not in waited:
                arrived(index_of[dx, dz, dy])
                waited.add(index_of[dx, dz, dy])
        left = wbuf[pl.ds(line * NY, NY)].reshape(NY * 16, kdim)
        total = None
        for side in (0, 1):
            rows = pl.ds(side * kdim, kdim)
            right = jnp.concatenate([fbuf[0, rows, :], fbuf[1, rows, :]], axis=1)
            d = dot(left, right).reshape(NY, 2, 8, 256)[:, side]
            total = d if total is None else total + d
        part[line] = total.reshape(NY * 8, 256)
        ahead = lax.rem(x - dx - r + 2 * NX, NR)
        place = lax.rem(z + dz, NZ)
        index = jnp.maximum(ahead - 1, 0)

        @pl.when(ahead != 0)
        def _():
            remote(
                part.at[line], rsbuf.at[index, place], rssend.at[line], rsrecv.at[index, place], peer(ahead)
            ).start()

        lines.append((line, ahead, index, place))

    for dx in PLANES:
        for dz in range(NZ):
            whiten(dx * NZ + dz)

    for k, rows in enumerate(halves):
        remote(fbuf.at[0, rows], fbuf.at[2, rows], fsend.at[1 + k], frecv.at[1 + k], blk(-sigma)).wait_recv()
        copy = remote(fbuf.at[2, rows], fbuf.at[3, rows], fsend.at[5 + k], frecv.at[5 + k], blk(2 * sigma))
        copy.start()
        pending.append(copy)

    row_id = lax.broadcasted_iota(jnp.int32, (128, 128), 0)
    lane_id = lax.broadcasted_iota(jnp.int32, (128, 128), 1)

    def exact(mask):
        return jnp.where(mask, 1.0, 0.0).astype(jnp.bfloat16)

    turns = [exact(row_id == pair_ref[s : s + 1, :]) for s in range(STEPS)]
    eye = exact(row_id == lane_id)
    swap_halves = exact(lax.rem(row_id + BLOCK, 2 * BLOCK) == lane_id)
    low_lane = lane_id < BLOCK
    first = jnp.where(low_lane, eye.astype(jnp.float32), turns[0].astype(jnp.float32)).astype(jnp.bfloat16)
    last = jnp.where(low_lane, eye.astype(jnp.float32), turns[3].astype(jnp.float32)).astype(jnp.bfloat16)
    across = (((1,), (1,)), ((), ()))
    down = (((0,), (0,)), ((), ()))
    q1, q2, q3 = (dot(turns[s - 1], turns[s], down).astype(jnp.bfloat16) for s in (1, 2, 3))
    for n, (b3, b2, b1) in enumerate(LEAVES):
        m = eye
        for bit, q in ((b3, q3), (b2, q2), (b1, q1)):
            if bit:
                m = dot(q, m).astype(jnp.bfloat16)
        e = dot(first, m)
        es = dot(e.astype(jnp.bfloat16), swap_halves)
        ebuf[n, :, 0:128] = e.astype(jnp.bfloat16)
        ebuf[n, :, 128:256] = es.astype(jnp.bfloat16)
        mbuf[n] = dot((e + es).astype(jnp.bfloat16), last, across)

    for k in range(3):
        for place in range(NZ):
            remote(part.at[0], rsbuf.at[k, place], rssend.at[0], rsrecv.at[k, place], peer(1)).wait_recv()
    for place in range(NZ):
        mine = lax.rem(x - r + NX, NX) * NZ + lax.rem(z + place, NZ)
        total = (part[mine] + rsbuf[0, place]) + (rsbuf[1, place] + rsbuf[2, place])
        wsum[0, place * 64 : place * 64 + 64, :] = total[:, 0:128]
        wsum[1, place * 64 : place * 64 + 64, :] = total[:, 128:256]

    for k, shift in enumerate((1, -1, 3, -3)):
        index = (3 - sigma * shift) // 2
        copy = remote(wsum.at[0], xbuf.at[index, core], xsend.at[k], xrecv.at[index, core], blk(sigma * shift))
        copy.start()
        pending.append(copy)
    for k, shift in enumerate((1, 3, -3)):
        index = (3 - sigma * shift) // 2
        copy = remote(
            wsum.at[1], xbuf.at[index, core], xsend.at[4 + k], xrecv.at[index, core], blk(sigma * (shift + 1))
        )
        copy.start()
        pending.append(copy)
    xbuf[(3 + sigma) // 2, core] = wsum[1]
    for shift in (1, -1, 3, -3):
        index = (3 + sigma * shift) // 2
        remote(wsum.at[0], xbuf.at[index, 1 - core], xsend.at[0], xrecv.at[index, 1 - core], blk(sigma)).wait_recv()
        if shift != 1:
            remote(wsum.at[0], xbuf.at[index, core], xsend.at[0], xrecv.at[index, core], blk(sigma)).wait_recv()

    for i in range(4):
        pieces = split3(xbuf[i].reshape(256, 128))
        for n in range(8):
            if sum(LEAVES[n]) == i:
                e = ebuf[n]
                ybuf[n] = dot(pieces[0], e) + dot(pieces[1], e) + dot(pieces[2], e)

    def put(name, a, c):
        k = GRAM[name]
        gram[k : k + 1, :] = jnp.sum(a * c, axis=0, keepdims=True)

    for n in range(8):
        a = ybuf[n, :, 0:128]
        put(("pr", n), a, a)
        put(("q", n), a, ybuf[n, :, 128:256])
        for m in range(8):
            if ("same", n, m) in GRAM:
                put(("same", n, m), a, ybuf[m, :, 0:128])
                put(("cross", n, m), a, ybuf[m, :, 128:256])
    gbuf[r] = gram[...]
    for shift in (1, 2, 3):
        copy = remote(gram, gbuf.at[r], gsend.at[shift - 1], grecv.at[r], peer(shift))
        copy.start()
        pending.append(copy)
    for shift in (1, 2, 3):
        other = lax.rem(r + shift, NR)
        remote(gram, gbuf.at[other], gsend.at[0], grecv.at[other], peer(shift)).wait_recv()
    gram_sum = (gbuf[0] + gbuf[1]) + (gbuf[2] + gbuf[3])
    gram_roll = pltpu.roll(gram_sum, BLOCK, 1)

    def row(name, rolled=False):
        k = GRAM[name]
        return (gram_roll if rolled else gram_sum)[k : k + 1, :]

    def rotate(node_u, node_l, p, rr, q):
        c, s = turn(p - rr, q)
        names = sorted(set(node_u) | set(node_l))
        up, low = {}, {}
        for name in names:
            if name in node_u and name in node_l:
                up[name] = c * node_u[name] + s * node_l[name]
                low[name] = c * node_l[name] - s * node_u[name]
            elif name in node_u:
                up[name] = c * node_u[name]
                low[name] = -s * node_u[name]
            else:
                up[name] = s * node_l[name]
                low[name] = c * node_l[name]
        cross = 2.0 * c * s * q
        return up, low, c * c * p + cross + s * s * rr, s * s * p - cross + c * c * rr

    def between(k1, k2):
        n, m = k1 // 2, k2 // 2
        if k1 % 2 == 0:
            return row(("same", n, m)) if k2 % 2 == 0 else row(("cross", n, m))
        return row(("cross", n, m), True) if k2 % 2 == 0 else row(("same", n, m), True)

    one = jnp.ones((1, 128), jnp.float32)
    nodes = [
        rotate({2 * n: one}, {2 * n + 1: one}, row(("pr", n)), row(("pr", n), True), row(("q", n))) for n in range(8)
    ]
    for level in (1, 2, 3):
        grown = []
        for k in range(0, len(nodes), 2):
            up, low = nodes[k][0], nodes[k + 1][1]
            q = None
            for k1, c1 in up.items():
                inner = None
                for k2, c2 in low.items():
                    term = c2 * between(k1, k2)
                    inner = term if inner is None else inner + term
                q = c1 * inner if q is None else q + c1 * inner
            grown.append(rotate(up, low, nodes[k][2], nodes[k + 1][3], q))
        nodes = grown
    up, low = nodes[0][0], nodes[0][1]
    low_row = lax.broadcasted_iota(jnp.int32, (1, 128), 1) < BLOCK
    for k in range(16):
        coef[k : k + 1, :] = jnp.where(low_row, up[k], pltpu.roll(low[k], BLOCK, 1))
    spread = sum(dot(piece, last, across) for piece in split3(coef[...]))
    upper_rows = row_id < BLOCK
    t = [None] * 4
    for n in range(8):
        term = mbuf[n] * jnp.where(upper_rows, spread[2 * n : 2 * n + 1, :], spread[2 * n + 1 : 2 * n + 2, :])
        i = sum(LEAVES[n])
        t[i] = term if t[i] is None else t[i] + term

    rotated = None
    pieces_t = [split3(v) for v in t]
    for i in range(4):
        xs = split3(xbuf[i].reshape(256, 128))
        for a in range(3):
            for c in range(3 - a):
                term = dot(xs[a], pieces_t[i][c])
                rotated = term if rotated is None else rotated + term
    for c in range(2):
        rot_ref[:, c] = rotated[c * 128 : c * 128 + 128].reshape(16, 8, 128)

    pair_t = [jnp.concatenate([v[0], v[1]], axis=1) for v in pieces_t]
    even = core == 0

    def choose(a, c):
        return jnp.where(even, a.astype(jnp.float32), c.astype(jnp.float32)).astype(jnp.bfloat16)

    t_cat = jnp.concatenate(
        [
            choose(pair_t[2], pair_t[1]),
            choose(pair_t[1], pair_t[2]),
            choose(pair_t[0], pair_t[3]),
            choose(pair_t[3], pair_t[0]),
        ],
        axis=0,
    )
    for k in range(2):
        remote(fbuf.at[0, halves[k]], fbuf.at[4, halves[k]], fsend.at[3 + k], frecv.at[3 + k], blk(sigma)).wait_recv()
        remote(fbuf.at[2, halves[k]], fbuf.at[3, halves[k]], fsend.at[5 + k], frecv.at[5 + k], blk(sigma)).wait_recv()

    def turn_rows(k, carry):
        rows = pl.ds(pl.multiple_of(k * 256, 256), 256)
        left = jnp.concatenate([fbuf[s, rows, :] for s in (1, 2, 3, 4)], axis=1)
        d = dot(left, t_cat)
        right_ref[rows, :] = d[:, 0:128] + d[:, 128:256]
        return carry

    lax.fori_loop(0, depth // 256, turn_rows, 0)

    for copy in pending:
        copy.wait_send()
    for line, ahead, index, place in lines:

        @pl.when(ahead != 0)
        def _():
            remote(
                part.at[line], rsbuf.at[index, place], rssend.at[line], rsrecv.at[index, place], peer(ahead)
            ).wait_send()


def per_device(weight, factor, pairing):
    pair = jnp.concatenate([pairing, pairing + BLOCK], axis=1)
    rows, depth = weight.shape
    vmem = pl.BlockSpec(memory_space=pltpu.VMEM)
    f32, b16 = jnp.float32, jnp.bfloat16
    dma = pltpu.SemaphoreType.DMA
    n_gram = len(GRAM)
    rotated, right = pl.pallas_call(
        kernel,
        out_shape=(jax.ShapeDtypeStruct((16, 2, 8, 128), f32), jax.ShapeDtypeStruct((depth, 128), f32)),
        in_specs=[vmem, pl.BlockSpec(memory_space=pl.ANY), vmem],
        out_specs=(vmem, vmem),
        scratch_shapes=[
            pltpu.VMEM((NX * NZ * NY, 2 * rows, depth // 2), b16),
            pltpu.VMEM((5, depth, 128), b16),
            pltpu.VMEM((NX * NZ, NY * rows, 256), f32),
            pltpu.VMEM((3, NZ, NY * rows, 256), f32),
            pltpu.VMEM((2, 128, 128), f32),
            pltpu.VMEM((4, 2, 128, 128), f32),
            pltpu.VMEM((8, 256, 256), f32),
            pltpu.VMEM((n_gram, 128), f32),
            pltpu.VMEM((4, n_gram, 128), f32),
            pltpu.VMEM((8, 128, 256), b16),
            pltpu.VMEM((8, 128, 128), f32),
            pltpu.VMEM((16, 128), f32),
            dma((len(TREE),)),
            dma((len(TREE),)),
            dma,
            dma((7,)),
            dma((7,)),
            dma((8,)),
            dma((3, NZ)),
            dma((7,)),
            dma((4, 2)),
            dma((3,)),
            dma((4,)),
        ],
        compiler_params=pltpu.CompilerParams(
            collective_id=0, has_side_effects=True, vmem_limit_bytes=48 * 2**20
        ),
        name="whiten_turn",
    )(weight, factor, pair)
    return rotated.reshape(256, 128), right


def solution(mesh):
    in_specs = (P("blk", "rows"), P("rows", "blk"), P())
    out_specs = (P("rows", "blk"), P("rows", "blk"))
    return jax.shard_map(per_device, mesh=mesh, in_specs=in_specs, out_specs=out_specs, check_vma=False)
```

```python
import functools
import jax
import jax.numpy as jnp
from jax import lax
from jax.experimental import pallas as pl
from jax.experimental.pallas import tpu as pltpu
from jax.sharding import PartitionSpec as P

MESH = pl.DeviceIdType.MESH
BLOCK = 64
STEPS = 4
NX, NZ, NY, NR = 4, 2, 8, 4
NB = 2 * NX * NZ * NY
HALF = NY // 2
HOPS = ((1, 0, 0), (3, 0, 0), (0, 1, 0), (0, 0, 1), (0, 0, 3))
TREE = (
    (0, 1, 0, 2), (3, 0, 0, 1), (1, 0, 0, 0), (0, 0, 3, 4), (0, 0, 1, 3), (2, 0, 0, 1), (1, 1, 0, 2), (3, 1, 0, 1),
    (1, 0, 3, 4), (0, 1, 1, 2), (1, 0, 1, 0), (3, 0, 3, 1), (2, 1, 0, 0), (0, 1, 3, 2), (3, 0, 1, 1), (0, 0, 2, 3),
    (1, 1, 1, 0), (2, 0, 3, 0), (2, 0, 1, 1), (0, 1, 2, 2), (1, 0, 2, 0), (3, 1, 1, 1), (2, 1, 1, 0), (3, 1, 3, 1),
    (2, 1, 3, 2), (3, 1, 2, 1), (2, 0, 2, 0), (1, 1, 2, 0), (1, 1, 3, 1), (2, 1, 2, 1), (3, 0, 2, 0),
)
LEAVES = tuple((b3, b2, b1) for b3 in (0, 1) for b2 in (0, 1) for b1 in (0, 1))


def plus(offset, hop):
    return tuple((a + b) % n for a, b, n in zip(offset, hop, (NX, NZ, HALF)))


def block_moves(which):
    sigma = 1 - 2 * (which % 2)
    pair = 1 - 2 * (which // 2)
    kinds, own = [], []
    for kind, base in enumerate((0, sigma, 2 * pair + sigma, 2 * pair)):
        moves = [(base + delta, (3 - delta) // 2) for delta in (1, -1, 3, -3)]
        own += [(kind, place) for shift, place in moves if shift == 0]
        kinds.append([(shift, place) for shift, place in moves if shift != 0])
    return kinds, own


MOVES = [block_moves(which) for which in range(4)]
SENDERS = [
    sorted(
        -shift
        for which in range(4)
        for kind in MOVES[which][0]
        for shift, _ in kind
        if (which + shift) % 4 == receiver
    )
    for receiver in range(4)
]


def turn(p_minus_r, q):
    y = 2.0 * q
    x = p_minus_r
    top = jnp.maximum(jnp.abs(x), jnp.abs(y))
    safe = jnp.where(top > 0.0, top, 1.0)
    xs = jnp.where(top > 0.0, x / safe, 1.0)
    ys = jnp.where(top > 0.0, y / safe, 0.0)
    h = jnp.sqrt(xs * xs + ys * ys)
    big = jnp.sqrt(0.5 * (1.0 + jnp.abs(xs) / h))
    small = jnp.abs(ys) / (2.0 * h * big)
    cosine = jnp.where(x >= 0.0, big, small)
    size = jnp.where(x >= 0.0, small, big)
    return cosine, jnp.where(y < 0.0, -size, size)


def split3(x):
    hi = x.astype(jnp.bfloat16)
    rest = x - hi.astype(jnp.float32)
    mid = rest.astype(jnp.bfloat16)
    low = (rest - mid.astype(jnp.float32)).astype(jnp.bfloat16)
    return hi, mid, low


def dot(a, b, dims=(((1,), (0,)), ((), ()))):
    return lax.dot_general(a, b, dims, preferred_element_type=jnp.float32)


def gram_plan():
    rows = {}
    for n in range(8):
        rows["pr", n] = len(rows)
        rows["q", n] = len(rows)
    for level in (1, 2, 3):
        for n in range(8):
            for m in range(8):
                if n >> level == m >> level and (n >> (level - 1)) & 1 == 0 and (m >> (level - 1)) & 1 == 1:
                    rows["same", n, m] = len(rows)
                    rows["cross", n, m] = len(rows)
    return rows


GRAM = gram_plan()


def kernel(
    w_hbm, f_ref, pair_hbm, rot_ref, right_ref,
    w_ref, pair_ref, wbuf, fbuf, part, rsbuf, part2, rsbuf2, wsum, xbuf, ybuf, gram, gbuf, ebuf, mbuf, coef,
    wsend, wrecv, w_sem, pair_sem, own_sem, fsend, frecv, rssend, rsrecv, rs2send, rs2recv, xsend, xrecv, gsend, grecv,
):
    b = lax.axis_index("blk")
    r = lax.axis_index("rows")
    core = lax.rem(b, 2)
    y = lax.rem(b // 2, NY)
    z = lax.rem(b // (2 * NY), NZ)
    x = b // (2 * NY * NZ)
    sigma = 1 - 2 * core
    odd = lax.rem(y, 2)
    yy = y // 2
    tau = sigma * (1 - 2 * odd)
    which = lax.rem(b, 4)

    def pick(values):
        if len(set(values)) == 1:
            return values[0]
        out = jnp.int32(values[0])
        for k in (1, 2, 3):
            out = jnp.where(which == k, values[k], out)
        return out

    def blk(shift):
        return (lax.rem(b + shift + NB, NB), r)

    def hop(h):
        dx, dz, dy = HOPS[h]
        index = lax.rem(x + dx, NX) * (2 * NY * NZ) + lax.rem(z + dz, NZ) * (2 * NY) + (lax.rem(yy + dy, HALF) * 2 + odd) * 2 + core
        return (index, r)

    def peer(shift):
        return (b, lax.rem(r + shift, NR))

    own_weight = pltpu.make_async_copy(w_hbm, w_ref, w_sem)
    own_weight.start()
    own_pairing = pltpu.make_async_copy(pair_hbm, pair_ref, pair_sem)
    own_pairing.start()
    own_factor = pltpu.make_async_copy(f_ref, fbuf.at[0], own_sem)
    own_factor.start()

    barrier = pltpu.get_barrier_semaphore()
    greet = [hop(h) for h in range(5)] + [peer(s) for s in (1, 2, 3)]
    greet += [blk(sigma * s) for s in (1, -1, 3, -3)]
    greet += [blk(pick([SENDERS[w][k] for w in range(4)])) for k in range(len(SENDERS[0]))]
    for target in greet:
        pl.semaphore_signal(barrier, inc=1, device_id=target, device_id_type=MESH)

    def remote(src, dst, send, recv, target):
        return pltpu.make_async_remote_copy(
            src_ref=src, dst_ref=dst, send_sem=send, recv_sem=recv, device_id=target, device_id_type=MESH
        )

    def slot(offset):
        return (offset[0] * NZ + offset[1]) * HALF + offset[2]

    index_of = {entry[:3]: k for k, entry in enumerate(TREE)}
    children = {}
    for k, entry in enumerate(TREE):
        back = tuple(-v for v in HOPS[entry[3]])
        children.setdefault(plus(entry[:3], back), []).append(k)
    pending = []

    def weight_copy(k):
        offset, h = TREE[k][:3], TREE[k][3]
        source = plus(offset, tuple(-v for v in HOPS[h]))
        return remote(wbuf.at[slot(source)], wbuf.at[slot(offset)], wsend.at[k], wrecv.at[k], hop(h))

    def forward(offset):
        for k in children.get(offset, ()):
            copy = weight_copy(k)
            copy.start()
            pending.append(copy)

    def arrived(k):
        weight_copy(k).wait_recv()

    own_weight.wait()
    wide = w_ref[...].astype(jnp.float32)
    half = wide.shape[1] // 2
    wbuf[0] = jnp.concatenate([wide[:, :half], wide[:, half:]], axis=0).astype(jnp.bfloat16)

    pl.semaphore_wait(barrier, len(greet))
    forward((0, 0, 0))
    own_factor.wait()
    swap = remote(fbuf.at[0], fbuf.at[1], fsend.at[0], frecv.at[0], blk(sigma))
    swap.start()
    pending.append(swap)

    depth = fbuf.shape[1]
    halves = [pl.ds(0, depth // 2), pl.ds(depth // 2, depth // 2)]
    moves = ((1, -1, 2), (3, 3, 4))
    near = jnp.where(tau > 0, 4, 2)

    def factor_copy(which_move, k):
        base, shift, place = moves[which_move]
        return remote(
            fbuf.at[0, halves[k]],
            fbuf.at[place, halves[k]],
            fsend.at[base + k],
            frecv.at[base + k],
            blk(sigma * shift),
        )

    def far_copy(k):
        return remote(
            fbuf.at[0, halves[k]], fbuf.at[3, halves[k]], fsend.at[5 + k], frecv.at[5 + k], blk(-3 * sigma)
        )

    def share_copy(k):
        return remote(fbuf.at[near, halves[k]], fbuf.at[5, halves[k]], fsend.at[7 + k], frecv.at[7 + k], blk(sigma))

    for k in (0, 1):
        for which_move in (0, 1):
            copy = factor_copy(which_move, k)
            copy.start()
            pending.append(copy)

    def share(k):
        @pl.when(tau > 0)
        def _():
            factor_copy(1, k).wait_recv()

        @pl.when(tau < 0)
        def _():
            factor_copy(0, k).wait_recv()

        copy = share_copy(k)
        copy.start()
        pending.append(copy)

    own_pairing.wait()

    row_id = lax.broadcasted_iota(jnp.int32, (128, 128), 0)
    lane_id = lax.broadcasted_iota(jnp.int32, (128, 128), 1)

    def exact(mask):
        return jnp.where(mask, 1.0, 0.0).astype(jnp.bfloat16)

    pairs = pair_ref[...]
    wide_pair = jnp.concatenate([pairs, pairs + BLOCK], axis=1)
    turns = [exact(row_id == wide_pair[s : s + 1, :]) for s in range(STEPS)]
    eye = exact(row_id == lane_id)
    swap_halves = exact(lax.rem(row_id + BLOCK, 2 * BLOCK) == lane_id)
    low_lane = lane_id < BLOCK
    first = jnp.where(low_lane, eye.astype(jnp.float32), turns[0].astype(jnp.float32)).astype(jnp.bfloat16)
    last = jnp.where(low_lane, eye.astype(jnp.float32), turns[3].astype(jnp.float32)).astype(jnp.bfloat16)
    across = (((1,), (1,)), ((), ()))
    down = (((0,), (0,)), ((), ()))
    q1, q2, q3 = (dot(turns[s - 1], turns[s], down).astype(jnp.bfloat16) for s in (1, 2, 3))
    for n, (b3, b2, b1) in enumerate(LEAVES):
        m = eye
        for bit, q in ((b3, q3), (b2, q2), (b1, q1)):
            if bit:
                m = dot(q, m).astype(jnp.bfloat16)
        e = dot(first, m)
        es = dot(e.astype(jnp.bfloat16), swap_halves)
        ebuf[n, :, 0:128] = e.astype(jnp.bfloat16)
        ebuf[n, :, 128:256] = es.astype(jnp.bfloat16)
        mbuf[n] = dot((e + es).astype(jnp.bfloat16), last, across)


    waited = set()
    kdim = half
    groups = []

    def product(left, first_block, second_block, sides):
        count = left.shape[0] // 16
        total = None
        for side in sides:
            rows = pl.ds(side * kdim, kdim)
            right = jnp.concatenate([fbuf[first_block, rows, :], fbuf[second_block, rows, :]], axis=1)
            d = dot(left, right).reshape(count, 2, 8, 256)[:, side]
            total = d if total is None else total + d
        return total.reshape(count * 8, 256)

    def send_sums(dx, src, dst, send, recv):
        ahead = lax.rem(x - dx - r + 2 * NX, NR)
        index = jnp.maximum(ahead - 1, 0)
        copy = remote(src, dst(index), send, recv(index), peer(ahead))

        @pl.when(ahead != 0)
        def _():
            copy.start()

        groups.append((ahead, copy))

    def whiten(line):
        dx, dz = line // NZ, line % NZ
        for dy in range(HALF):
            if (dx, dz, dy) != (0, 0, 0) and index_of[dx, dz, dy] not in waited:
                arrived(index_of[dx, dz, dy])
                waited.add(index_of[dx, dz, dy])
        left = wbuf[pl.ds(line * HALF, HALF)].reshape(HALF * 16, kdim)
        part[line] = product(left, 0, 1, (0, 1))
        send_sums(
            dx,
            part.at[line],
            lambda index: rsbuf.at[index, dz],
            rssend.at[line],
            lambda index: rsrecv.at[index, dz],
        )

    mine = lax.rem(x - r + NX, NX)

    def row_place(dz, dy):
        at = lax.rem(z + dz, NZ) * 32 + lax.rem(yy - dy + HALF, HALF) * 8
        return pl.ds(pl.multiple_of(at, 8), 8)

    def sum_own():
        for dz in range(NZ):
            for k in range(3):
                remote(part.at[0], rsbuf.at[k, dz], rssend.at[0], rsrecv.at[k, dz], peer(1)).wait_recv()
            total = (part[mine * NZ + dz] + rsbuf[0, dz]) + (rsbuf[1, dz] + rsbuf[2, dz])
            for dy in range(HALF):
                wsum[0, row_place(dz, dy), :] = total[8 * dy : 8 * dy + 8, 0:128]
                wsum[1, row_place(dz, dy), :] = total[8 * dy : 8 * dy + 8, 128:256]

    def whiten_partner(dx):
        left = wbuf[pl.ds(dx * NZ * HALF, NZ * HALF)].reshape(NZ * HALF * 16, kdim)
        part2[dx] = product(left, near, 5, (0, 1))
        send_sums(dx, part2.at[dx], lambda index: rsbuf2.at[index], rs2send.at[dx], lambda index: rs2recv.at[index])

    def sum_partner():
        for k in range(3):
            remote(part2.at[0], rsbuf2.at[k], rs2send.at[0], rs2recv.at[k], peer(1)).wait_recv()
        total = (part2[mine] + rsbuf2[0]) + (rsbuf2[1] + rsbuf2[2])
        for dz in range(NZ):
            for dy in range(HALF):
                at = (dz * HALF + dy) * 8
                wsum[2, row_place(dz, dy), :] = total[at : at + 8, 0:128]
                wsum[3, row_place(dz, dy), :] = total[at : at + 8, 128:256]

    def block_out(kinds):
        for kind in kinds:
            for k in range(len(MOVES[0][0][kind])):
                shift = pick([MOVES[w][0][kind][k][0] for w in range(4)])
                place = pick([MOVES[w][0][kind][k][1] for w in range(4)])
                copy = remote(
                    wsum.at[kind],
                    xbuf.at[place, core, odd],
                    xsend.at[kind, k],
                    xrecv.at[place, core, odd],
                    blk(shift),
                )
                copy.start()
                pending.append(copy)
            for k in range(2):
                if MOVES[0][1][k][0] == kind:
                    place = pick([MOVES[w][1][k][1] for w in range(4)])
                    xbuf[place, core, odd] = wsum[kind]

    events = []
    for line in range(NX * NZ):
        last_index = max(index_of.get((line // NZ, line % NZ, dy), -1) for dy in range(HALF))
        events.append((last_index, 1, line))
    for k, entry in enumerate(TREE):
        if entry[:3] in children:
            events.append((k, 0, k))
    events.sort()
    begun = False
    for _, kind, a in events:
        if kind == 0:
            arrived(a)
            waited.add(a)
            forward(TREE[a][:3])
        else:
            if not begun:
                swap.wait_recv()
                begun = True
            whiten(a)
    for k in (0, 1):
        copy = far_copy(k)
        copy.start()
        pending.append(copy)
    for k in (0, 1):
        share(k)
    sum_own()
    block_out((0, 1))
    for k in (0, 1):
        share_copy(k).wait_recv()
    for dx in range(NX):
        whiten_partner(dx)
    sum_partner()
    block_out((2, 3))
    taken = [pick([MOVES[w][1][k][1] for w in range(4)]) for k in range(2)]
    for place in range(4):
        for kind in range(2):
            for side in range(2):
                here = jnp.logical_and(kind == core, side == odd)
                here = jnp.logical_and(here, jnp.logical_or(place == taken[0], place == taken[1]))

                @pl.when(jnp.logical_not(here))
                def _():
                    remote(
                        wsum.at[0], xbuf.at[place, kind, side], xsend.at[0, 0], xrecv.at[place, kind, side], blk(sigma)
                    ).wait_recv()

    for i in range(4):
        pieces = split3(xbuf[i].reshape(256, 128))
        for n in range(8):
            if sum(LEAVES[n]) == i:
                e = ebuf[n]
                ybuf[n] = dot(pieces[0], e) + dot(pieces[1], e) + dot(pieces[2], e)

    def put(name, a, c):
        k = GRAM[name]
        gram[k : k + 1, :] = jnp.sum(a * c, axis=0, keepdims=True)

    for n in range(8):
        a = ybuf[n, :, 0:128]
        put(("pr", n), a, a)
        put(("q", n), a, ybuf[n, :, 128:256])
        for m in range(8):
            if ("same", n, m) in GRAM:
                put(("same", n, m), a, ybuf[m, :, 0:128])
                put(("cross", n, m), a, ybuf[m, :, 128:256])
    gbuf[r] = gram[...]
    for shift in (1, 2, 3):
        copy = remote(gram, gbuf.at[r], gsend.at[shift - 1], grecv.at[r], peer(shift))
        copy.start()
        pending.append(copy)
    for shift in (1, 2, 3):
        other = lax.rem(r + shift, NR)
        remote(gram, gbuf.at[other], gsend.at[0], grecv.at[other], peer(shift)).wait_recv()
    gram_sum = (gbuf[0] + gbuf[1]) + (gbuf[2] + gbuf[3])
    gram_roll = pltpu.roll(gram_sum, BLOCK, 1)

    def row(name, rolled=False):
        k = GRAM[name]
        return (gram_roll if rolled else gram_sum)[k : k + 1, :]

    def rotate(node_u, node_l, p, rr, q):
        c, s = turn(p - rr, q)
        names = sorted(set(node_u) | set(node_l))
        up, low = {}, {}
        for name in names:
            if name in node_u and name in node_l:
                up[name] = c * node_u[name] + s * node_l[name]
                low[name] = c * node_l[name] - s * node_u[name]
            elif name in node_u:
                up[name] = c * node_u[name]
                low[name] = -s * node_u[name]
            else:
                up[name] = s * node_l[name]
                low[name] = c * node_l[name]
        cross = 2.0 * c * s * q
        return up, low, c * c * p + cross + s * s * rr, s * s * p - cross + c * c * rr

    def between(k1, k2):
        n, m = k1 // 2, k2 // 2
        if k1 % 2 == 0:
            return row(("same", n, m)) if k2 % 2 == 0 else row(("cross", n, m))
        return row(("cross", n, m), True) if k2 % 2 == 0 else row(("same", n, m), True)

    one = jnp.ones((1, 128), jnp.float32)
    nodes = [
        rotate({2 * n: one}, {2 * n + 1: one}, row(("pr", n)), row(("pr", n), True), row(("q", n))) for n in range(8)
    ]
    for level in (1, 2, 3):
        grown = []
        for k in range(0, len(nodes), 2):
            up, low = nodes[k][0], nodes[k + 1][1]
            q = None
            for k1, c1 in up.items():
                inner = None
                for k2, c2 in low.items():
                    term = c2 * between(k1, k2)
                    inner = term if inner is None else inner + term
                q = c1 * inner if q is None else q + c1 * inner
            grown.append(rotate(up, low, nodes[k][2], nodes[k + 1][3], q))
        nodes = grown
    up, low = nodes[0][0], nodes[0][1]
    low_row = lax.broadcasted_iota(jnp.int32, (1, 128), 1) < BLOCK
    for k in range(16):
        coef[k : k + 1, :] = jnp.where(low_row, up[k], pltpu.roll(low[k], BLOCK, 1))
    spread = sum(dot(piece, last, across) for piece in split3(coef[...]))
    upper_rows = row_id < BLOCK
    t = [None] * 4
    for n in range(8):
        term = mbuf[n] * jnp.where(upper_rows, spread[2 * n : 2 * n + 1, :], spread[2 * n + 1 : 2 * n + 2, :])
        i = sum(LEAVES[n])
        t[i] = term if t[i] is None else t[i] + term

    rotated = None
    pieces_t = [split3(v) for v in t]
    for i in range(4):
        xs = split3(xbuf[i].reshape(256, 128))
        for a in range(3):
            for c in range(3 - a):
                term = dot(xs[a], pieces_t[i][c])
                rotated = term if rotated is None else rotated + term
    for c in range(2):
        for side in range(2):
            at = (c * 2 + side) * 64
            rot_ref[:, side, c] = rotated[at : at + 64].reshape(8, 8, 128)

    pair_t = [jnp.concatenate([v[0], v[1]], axis=1) for v in pieces_t]
    even = core == 0

    def choose(a, c):
        return jnp.where(even, a.astype(jnp.float32), c.astype(jnp.float32)).astype(jnp.bfloat16)

    t_cat = jnp.concatenate(
        [
            choose(pair_t[2], pair_t[1]),
            choose(pair_t[1], pair_t[2]),
            choose(pair_t[0], pair_t[3]),
            choose(pair_t[3], pair_t[0]),
        ],
        axis=0,
    )
    for k in (0, 1):

        @pl.when(tau < 0)
        def _():
            factor_copy(1, k).wait_recv()

        @pl.when(tau > 0)
        def _():
            factor_copy(0, k).wait_recv()

        far_copy(k).wait_recv()

    def turn_rows(k, carry):
        rows = pl.ds(pl.multiple_of(k * 512, 512), 512)
        left = jnp.concatenate([fbuf[s, rows, :] for s in (1, 2, 3, 4)], axis=1)
        d = dot(left, t_cat)
        right_ref[rows, :] = d[:, 0:128] + d[:, 128:256]
        return carry

    lax.fori_loop(0, depth // 512, turn_rows, 0)

    for copy in pending:
        copy.wait_send()
    for ahead, copy in groups:

        @pl.when(ahead != 0)
        def _():
            copy.wait_send()


def per_device(weight, factor, pairing):
    rows, depth = weight.shape
    vmem = pl.BlockSpec(memory_space=pltpu.VMEM)
    f32, b16 = jnp.float32, jnp.bfloat16
    dma = pltpu.SemaphoreType.DMA
    n_gram = len(GRAM)
    rotated, right = pl.pallas_call(
        kernel,
        out_shape=(jax.ShapeDtypeStruct((8, 2, 2, 8, 128), f32), jax.ShapeDtypeStruct((depth, 128), f32)),
        in_specs=[pl.BlockSpec(memory_space=pltpu.HBM)] * 3,
        out_specs=(vmem, vmem),
        scratch_shapes=[
            pltpu.VMEM((rows, depth), b16),
            pltpu.VMEM(pairing.shape, jnp.int32),
            pltpu.VMEM((NX * NZ * HALF, 2 * rows, depth // 2), b16),
            pltpu.VMEM((6, depth, 128), b16),
            pltpu.VMEM((NX * NZ, HALF * rows, 256), f32),
            pltpu.VMEM((3, NZ, HALF * rows, 256), f32),
            pltpu.VMEM((NX, NZ * HALF * rows, 256), f32),
            pltpu.VMEM((3, NZ * HALF * rows, 256), f32),
            pltpu.VMEM((4, 64, 128), f32),
            pltpu.VMEM((4, 2, 2, 64, 128), f32),
            pltpu.VMEM((8, 256, 256), f32),
            pltpu.VMEM((n_gram, 128), f32),
            pltpu.VMEM((4, n_gram, 128), f32),
            pltpu.VMEM((8, 128, 256), b16),
            pltpu.VMEM((8, 128, 128), f32),
            pltpu.VMEM((16, 128), f32),
            dma((len(TREE),)),
            dma((len(TREE),)),
            dma,
            dma,
            dma,
            dma((9,)),
            dma((9,)),
            dma((NX * NZ,)),
            dma((3, NZ)),
            dma((NX,)),
            dma((3,)),
            dma((4, 4)),
            dma((4, 2, 2)),
            dma((3,)),
            dma((4,)),
        ],
        compiler_params=pltpu.CompilerParams(
            collective_id=0, has_side_effects=True, vmem_limit_bytes=60 * 2**20
        ),
        name="whiten_turn",
    )(weight, factor, pairing)
    return rotated.reshape(256, 128), right


def solution(mesh):
    in_specs = (P("blk", "rows"), P("rows", "blk"), P())
    out_specs = (P("rows", "blk"), P("rows", "blk"))
    return jax.shard_map(per_device, mesh=mesh, in_specs=in_specs, out_specs=out_specs, check_vma=False)
```

```python
import functools
import jax
import jax.numpy as jnp
from jax import lax
from jax.experimental import pallas as pl
from jax.experimental.pallas import tpu as pltpu
from jax.sharding import PartitionSpec as P

MESH = pl.DeviceIdType.MESH
BLOCK = 64
STEPS = 4
NX, NZ, NY, NR = 4, 2, 8, 4
NB = 2 * NX * NZ * NY
HALF = NY // 2
HOPS = ((1, 0, 0), (3, 0, 0), (0, 1, 0), (0, 0, 1), (0, 0, 3))
TREE = (
    (0, 1, 0, 2), (3, 0, 0, 1), (1, 0, 0, 0), (0, 0, 3, 4), (0, 0, 1, 3), (2, 0, 0, 1), (1, 1, 0, 2), (3, 1, 0, 1),
    (1, 0, 3, 4), (0, 1, 1, 2), (1, 0, 1, 0), (3, 0, 3, 1), (2, 1, 0, 0), (0, 1, 3, 2), (3, 0, 1, 1), (0, 0, 2, 3),
    (1, 1, 1, 0), (2, 0, 3, 0), (2, 0, 1, 1), (0, 1, 2, 2), (1, 0, 2, 0), (3, 1, 1, 1), (2, 1, 1, 0), (3, 1, 3, 1),
    (2, 1, 3, 2), (3, 1, 2, 1), (2, 0, 2, 0), (1, 1, 2, 0), (1, 1, 3, 1), (2, 1, 2, 1), (3, 0, 2, 0),
)
LEAVES = tuple((b3, b2, b1) for b3 in (0, 1) for b2 in (0, 1) for b1 in (0, 1))


def plus(offset, hop):
    return tuple((a + b) % n for a, b, n in zip(offset, hop, (NX, NZ, HALF)))


def block_moves(which):
    sigma = 1 - 2 * (which % 2)
    pair = 1 - 2 * (which // 2)
    kinds, own = [], []
    for kind, base in enumerate((0, sigma, 2 * pair + sigma, 2 * pair)):
        moves = [(base + delta, (3 - delta) // 2) for delta in (1, -1, 3, -3)]
        own += [(kind, place) for shift, place in moves if shift == 0]
        kinds.append([(shift, place) for shift, place in moves if shift != 0])
    return kinds, own


MOVES = [block_moves(which) for which in range(4)]
SENDERS = [
    sorted(
        -shift
        for which in range(4)
        for kind in MOVES[which][0]
        for shift, _ in kind
        if (which + shift) % 4 == receiver
    )
    for receiver in range(4)
]


def turn(p_minus_r, q):
    y = 2.0 * q
    x = p_minus_r
    top = jnp.maximum(jnp.abs(x), jnp.abs(y))
    safe = jnp.where(top > 0.0, top, 1.0)
    xs = jnp.where(top > 0.0, x / safe, 1.0)
    ys = jnp.where(top > 0.0, y / safe, 0.0)
    h = jnp.sqrt(xs * xs + ys * ys)
    big = jnp.sqrt(0.5 * (1.0 + jnp.abs(xs) / h))
    small = jnp.abs(ys) / (2.0 * h * big)
    cosine = jnp.where(x >= 0.0, big, small)
    size = jnp.where(x >= 0.0, small, big)
    return cosine, jnp.where(y < 0.0, -size, size)


def split3(x):
    hi = x.astype(jnp.bfloat16)
    rest = x - hi.astype(jnp.float32)
    mid = rest.astype(jnp.bfloat16)
    low = (rest - mid.astype(jnp.float32)).astype(jnp.bfloat16)
    return hi, mid, low


def dot(a, b, dims=(((1,), (0,)), ((), ()))):
    return lax.dot_general(a, b, dims, preferred_element_type=jnp.float32)


def gram_plan():
    rows = {}
    for n in range(8):
        rows["pr", n] = len(rows)
        rows["q", n] = len(rows)
    for level in (1, 2, 3):
        for n in range(8):
            for m in range(8):
                if n >> level == m >> level and (n >> (level - 1)) & 1 == 0 and (m >> (level - 1)) & 1 == 1:
                    rows["same", n, m] = len(rows)
                    rows["cross", n, m] = len(rows)
    return rows


GRAM = gram_plan()


def kernel(
    w_hbm, f_ref, pair_hbm, rot_ref, right_ref,
    w_ref, pair_ref, wbuf, fbuf, part, rsbuf, part2, rsbuf2, wsum, xbuf, ybuf, gram, gbuf, ebuf, mbuf, coef,
    wsend, wrecv, w_sem, pair_sem, own_sem, fsend, frecv, rssend, rsrecv, rs2send, rs2recv, xsend, xrecv, gsend, grecv,
):
    b = lax.axis_index("blk")
    r = lax.axis_index("rows")
    core = lax.rem(b, 2)
    y = lax.rem(b // 2, NY)
    z = lax.rem(b // (2 * NY), NZ)
    x = b // (2 * NY * NZ)
    sigma = 1 - 2 * core
    odd = lax.rem(y, 2)
    yy = y // 2
    tau = sigma * (1 - 2 * odd)
    which = lax.rem(b, 4)

    def pick(values):
        if len(set(values)) == 1:
            return values[0]
        out = jnp.int32(values[0])
        for k in (1, 2, 3):
            out = jnp.where(which == k, values[k], out)
        return out

    def blk(shift):
        return (lax.rem(b + shift + NB, NB), r)

    def hop(h):
        dx, dz, dy = HOPS[h]
        index = lax.rem(x + dx, NX) * (2 * NY * NZ) + lax.rem(z + dz, NZ) * (2 * NY) + (lax.rem(yy + dy, HALF) * 2 + odd) * 2 + core
        return (index, r)

    def peer(shift):
        return (b, lax.rem(r + shift, NR))

    own_weight = pltpu.make_async_copy(w_hbm, w_ref, w_sem)
    own_weight.start()
    own_pairing = pltpu.make_async_copy(pair_hbm, pair_ref, pair_sem)
    own_pairing.start()
    own_factor = pltpu.make_async_copy(f_ref, fbuf.at[0], own_sem)
    own_factor.start()

    barrier = pltpu.get_barrier_semaphore()
    greet = [hop(h) for h in range(5)] + [peer(s) for s in (1, 2, 3)]
    greet += [blk(sigma * s) for s in (1, -1, 3, -3)]
    greet += [blk(pick([SENDERS[w][k] for w in range(4)])) for k in range(len(SENDERS[0]))]
    for target in greet:
        pl.semaphore_signal(barrier, inc=1, device_id=target, device_id_type=MESH)

    def remote(src, dst, send, recv, target):
        return pltpu.make_async_remote_copy(
            src_ref=src, dst_ref=dst, send_sem=send, recv_sem=recv, device_id=target, device_id_type=MESH
        )

    def slot(offset):
        return (offset[0] * NZ + offset[1]) * HALF + offset[2]

    index_of = {entry[:3]: k for k, entry in enumerate(TREE)}
    children = {}
    for k, entry in enumerate(TREE):
        back = tuple(-v for v in HOPS[entry[3]])
        children.setdefault(plus(entry[:3], back), []).append(k)
    pending = []

    def weight_copy(k):
        offset, h = TREE[k][:3], TREE[k][3]
        source = plus(offset, tuple(-v for v in HOPS[h]))
        return remote(wbuf.at[slot(source)], wbuf.at[slot(offset)], wsend.at[k], wrecv.at[k], hop(h))

    def forward(offset):
        for k in children.get(offset, ()):
            copy = weight_copy(k)
            copy.start()
            pending.append(copy)

    def arrived(k):
        weight_copy(k).wait_recv()

    own_weight.wait()
    wide = w_ref[...].astype(jnp.float32)
    half = wide.shape[1] // 2
    wbuf[0] = jnp.concatenate([wide[:, :half], wide[:, half:]], axis=0).astype(jnp.bfloat16)

    pl.semaphore_wait(barrier, len(greet))
    forward((0, 0, 0))
    own_factor.wait()
    swap = remote(fbuf.at[0], fbuf.at[1], fsend.at[0], frecv.at[0], blk(sigma))
    swap.start()
    pending.append(swap)

    depth = fbuf.shape[1]
    halves = [pl.ds(0, depth // 2), pl.ds(depth // 2, depth // 2)]
    moves = ((1, -1, 2), (3, 3, 4))
    near = jnp.where(tau > 0, 4, 2)

    def factor_copy(which_move, k):
        base, shift, place = moves[which_move]
        return remote(
            fbuf.at[0, halves[k]],
            fbuf.at[place, halves[k]],
            fsend.at[base + k],
            frecv.at[base + k],
            blk(sigma * shift),
        )

    def far_copy(k):
        return remote(
            fbuf.at[0, halves[k]], fbuf.at[3, halves[k]], fsend.at[5 + k], frecv.at[5 + k], blk(-3 * sigma)
        )

    def share_copy(k):
        return remote(fbuf.at[near, halves[k]], fbuf.at[5, halves[k]], fsend.at[7 + k], frecv.at[7 + k], blk(sigma))

    for k in (0, 1):
        for which_move in (0, 1):
            copy = factor_copy(which_move, k)
            copy.start()
            pending.append(copy)

    def share(k):
        @pl.when(tau > 0)
        def _():
            factor_copy(1, k).wait_recv()

        @pl.when(tau < 0)
        def _():
            factor_copy(0, k).wait_recv()

        copy = share_copy(k)
        copy.start()
        pending.append(copy)

    own_pairing.wait()

    row_id = lax.broadcasted_iota(jnp.int32, (128, 128), 0)
    lane_id = lax.broadcasted_iota(jnp.int32, (128, 128), 1)

    def exact(mask):
        return jnp.where(mask, 1.0, 0.0).astype(jnp.bfloat16)

    pairs = pair_ref[...]
    wide_pair = jnp.concatenate([pairs, pairs + BLOCK], axis=1)
    turns = [exact(row_id == wide_pair[s : s + 1, :]) for s in range(STEPS)]
    eye = exact(row_id == lane_id)
    swap_halves = exact(lax.rem(row_id + BLOCK, 2 * BLOCK) == lane_id)
    low_lane = lane_id < BLOCK
    first = jnp.where(low_lane, eye.astype(jnp.float32), turns[0].astype(jnp.float32)).astype(jnp.bfloat16)
    last = jnp.where(low_lane, eye.astype(jnp.float32), turns[3].astype(jnp.float32)).astype(jnp.bfloat16)
    across = (((1,), (1,)), ((), ()))
    down = (((0,), (0,)), ((), ()))
    q1, q2, q3 = (dot(turns[s - 1], turns[s], down).astype(jnp.bfloat16) for s in (1, 2, 3))
    for n, (b3, b2, b1) in enumerate(LEAVES):
        m = eye
        for bit, q in ((b3, q3), (b2, q2), (b1, q1)):
            if bit:
                m = dot(q, m).astype(jnp.bfloat16)
        e = dot(first, m)
        es = dot(e.astype(jnp.bfloat16), swap_halves)
        ebuf[n, :, 0:128] = e.astype(jnp.bfloat16)
        ebuf[n, :, 128:256] = es.astype(jnp.bfloat16)
        mbuf[n] = dot((e + es).astype(jnp.bfloat16), last, across)


    waited = set()
    kdim = half
    groups = []

    def product(left, first_block, second_block, sides):
        count = left.shape[0] // 16
        total = None
        for side in sides:
            rows = pl.ds(side * kdim, kdim)
            right = jnp.concatenate([fbuf[first_block, rows, :], fbuf[second_block, rows, :]], axis=1)
            d = dot(left, right).reshape(count, 2, 8, 256)[:, side]
            total = d if total is None else total + d
        return total.reshape(count * 8, 256)

    def send_sums(dx, src, dst, send, recv):
        ahead = lax.rem(x - dx - r + 2 * NX, NR)
        index = jnp.maximum(ahead - 1, 0)
        copy = remote(src, dst(index), send, recv(index), peer(ahead))

        @pl.when(ahead != 0)
        def _():
            copy.start()

        groups.append((ahead, copy))

    def whiten(line):
        dx, dz = line // NZ, line % NZ
        for dy in range(HALF):
            if (dx, dz, dy) != (0, 0, 0) and index_of[dx, dz, dy] not in waited:
                arrived(index_of[dx, dz, dy])
                waited.add(index_of[dx, dz, dy])
        left = wbuf[pl.ds(line * HALF, HALF)].reshape(HALF * 16, kdim)
        part[line] = product(left, 0, 1, (0, 1))
        send_sums(
            dx,
            part.at[line],
            lambda index: rsbuf.at[index, dz],
            rssend.at[line],
            lambda index: rsrecv.at[index, dz],
        )

    mine = lax.rem(x - r + NX, NX)

    def row_place(dz, dy):
        at = lax.rem(z + dz, NZ) * 32 + lax.rem(yy - dy + HALF, HALF) * 8
        return pl.ds(pl.multiple_of(at, 8), 8)

    def sum_own():
        for dz in range(NZ):
            for k in range(3):
                remote(part.at[0], rsbuf.at[k, dz], rssend.at[0], rsrecv.at[k, dz], peer(1)).wait_recv()
            total = (part[mine * NZ + dz] + rsbuf[0, dz]) + (rsbuf[1, dz] + rsbuf[2, dz])
            for dy in range(HALF):
                wsum[0, row_place(dz, dy), :] = total[8 * dy : 8 * dy + 8, 0:128]
                wsum[1, row_place(dz, dy), :] = total[8 * dy : 8 * dy + 8, 128:256]

    def whiten_partner(dx):
        left = wbuf[pl.ds(dx * NZ * HALF, NZ * HALF)].reshape(NZ * HALF * 16, kdim)
        part2[dx] = product(left, near, 5, (0, 1))
        send_sums(dx, part2.at[dx], lambda index: rsbuf2.at[index], rs2send.at[dx], lambda index: rs2recv.at[index])

    def sum_partner():
        for k in range(3):
            remote(part2.at[0], rsbuf2.at[k], rs2send.at[0], rs2recv.at[k], peer(1)).wait_recv()
        total = (part2[mine] + rsbuf2[0]) + (rsbuf2[1] + rsbuf2[2])
        for dz in range(NZ):
            for dy in range(HALF):
                at = (dz * HALF + dy) * 8
                wsum[2, row_place(dz, dy), :] = total[at : at + 8, 0:128]
                wsum[3, row_place(dz, dy), :] = total[at : at + 8, 128:256]

    def block_out(kinds):
        for kind in kinds:
            for k in range(len(MOVES[0][0][kind])):
                shift = pick([MOVES[w][0][kind][k][0] for w in range(4)])
                place = pick([MOVES[w][0][kind][k][1] for w in range(4)])
                copy = remote(
                    wsum.at[kind],
                    xbuf.at[place, core, odd],
                    xsend.at[kind, k],
                    xrecv.at[place, core, odd],
                    blk(shift),
                )
                copy.start()
                pending.append(copy)
            for k in range(2):
                if MOVES[0][1][k][0] == kind:
                    place = pick([MOVES[w][1][k][1] for w in range(4)])
                    xbuf[place, core, odd] = wsum[kind]

    events = []
    for line in range(NX * NZ):
        last_index = max(index_of.get((line // NZ, line % NZ, dy), -1) for dy in range(HALF))
        events.append((last_index, 1, line))
    for k, entry in enumerate(TREE):
        if entry[:3] in children:
            events.append((k, 0, k))
    events.sort()
    begun = False
    for _, kind, a in events:
        if kind == 0:
            arrived(a)
            waited.add(a)
            forward(TREE[a][:3])
        else:
            if not begun:
                swap.wait_recv()
                begun = True
            whiten(a)
    for k in (0, 1):
        copy = far_copy(k)
        copy.start()
        pending.append(copy)
    for k in (0, 1):
        share(k)
    sum_own()
    block_out((0, 1))
    for k in (0, 1):
        share_copy(k).wait_recv()
    for dx in range(NX):
        whiten_partner(dx)
    sum_partner()
    block_out((2, 3))
    taken = [pick([MOVES[w][1][k][1] for w in range(4)]) for k in range(2)]
    for place in range(4):
        for kind in range(2):
            for side in range(2):
                here = jnp.logical_and(kind == core, side == odd)
                here = jnp.logical_and(here, jnp.logical_or(place == taken[0], place == taken[1]))

                @pl.when(jnp.logical_not(here))
                def _():
                    remote(
                        wsum.at[0], xbuf.at[place, kind, side], xsend.at[0, 0], xrecv.at[place, kind, side], blk(sigma)
                    ).wait_recv()

    for i in range(4):
        pieces = split3(xbuf[i].reshape(256, 128))
        for n in range(8):
            if sum(LEAVES[n]) == i:
                e = ebuf[n]
                ybuf[n] = dot(pieces[0], e) + dot(pieces[1], e) + dot(pieces[2], e)

    def put(name, a, c):
        k = GRAM[name]
        gram[k : k + 1, :] = jnp.sum(a * c, axis=0, keepdims=True)

    for n in range(8):
        a = ybuf[n, :, 0:128]
        put(("pr", n), a, a)
        put(("q", n), a, ybuf[n, :, 128:256])
        for m in range(8):
            if ("same", n, m) in GRAM:
                put(("same", n, m), a, ybuf[m, :, 0:128])
                put(("cross", n, m), a, ybuf[m, :, 128:256])
    gbuf[r] = gram[...]
    for shift in (1, 2, 3):
        copy = remote(gram, gbuf.at[r], gsend.at[shift - 1], grecv.at[r], peer(shift))
        copy.start()
        pending.append(copy)
    for shift in (1, 2, 3):
        other = lax.rem(r + shift, NR)
        remote(gram, gbuf.at[other], gsend.at[0], grecv.at[other], peer(shift)).wait_recv()
    gram_sum = (gbuf[0] + gbuf[1]) + (gbuf[2] + gbuf[3])
    gram_roll = pltpu.roll(gram_sum, BLOCK, 1)

    def row(name, rolled=False):
        k = GRAM[name]
        return (gram_roll if rolled else gram_sum)[k : k + 1, :]

    def rotate(node_u, node_l, p, rr, q):
        c, s = turn(p - rr, q)
        names = sorted(set(node_u) | set(node_l))
        up, low = {}, {}
        for name in names:
            if name in node_u and name in node_l:
                up[name] = c * node_u[name] + s * node_l[name]
                low[name] = c * node_l[name] - s * node_u[name]
            elif name in node_u:
                up[name] = c * node_u[name]
                low[name] = -s * node_u[name]
            else:
                up[name] = s * node_l[name]
                low[name] = c * node_l[name]
        cross = 2.0 * c * s * q
        return up, low, c * c * p + cross + s * s * rr, s * s * p - cross + c * c * rr

    def between(k1, k2):
        n, m = k1 // 2, k2 // 2
        if k1 % 2 == 0:
            return row(("same", n, m)) if k2 % 2 == 0 else row(("cross", n, m))
        return row(("cross", n, m), True) if k2 % 2 == 0 else row(("same", n, m), True)

    one = jnp.ones((1, 128), jnp.float32)
    nodes = [
        rotate({2 * n: one}, {2 * n + 1: one}, row(("pr", n)), row(("pr", n), True), row(("q", n))) for n in range(8)
    ]
    for level in (1, 2, 3):
        grown = []
        for k in range(0, len(nodes), 2):
            up, low = nodes[k][0], nodes[k + 1][1]
            q = None
            for k1, c1 in up.items():
                inner = None
                for k2, c2 in low.items():
                    term = c2 * between(k1, k2)
                    inner = term if inner is None else inner + term
                q = c1 * inner if q is None else q + c1 * inner
            grown.append(rotate(up, low, nodes[k][2], nodes[k + 1][3], q))
        nodes = grown
    up, low = nodes[0][0], nodes[0][1]
    low_row = lax.broadcasted_iota(jnp.int32, (1, 128), 1) < BLOCK
    for k in range(16):
        coef[k : k + 1, :] = jnp.where(low_row, up[k], pltpu.roll(low[k], BLOCK, 1))
    spread = sum(dot(piece, last, across) for piece in split3(coef[...]))
    upper_rows = row_id < BLOCK
    t = [None] * 4
    for n in range(8):
        term = mbuf[n] * jnp.where(upper_rows, spread[2 * n : 2 * n + 1, :], spread[2 * n + 1 : 2 * n + 2, :])
        i = sum(LEAVES[n])
        t[i] = term if t[i] is None else t[i] + term

    rotated = None
    pieces_t = [split3(v) for v in t]
    for i in range(4):
        xs = split3(xbuf[i].reshape(256, 128))
        for a in range(3):
            for c in range(3 - a):
                term = dot(xs[a], pieces_t[i][c])
                rotated = term if rotated is None else rotated + term
    for c in range(2):
        for side in range(2):
            at = (c * 2 + side) * 64
            rot_ref[:, side, c] = rotated[at : at + 64].reshape(8, 8, 128)

    pair_t = [jnp.concatenate([v[0], v[1]], axis=1) for v in pieces_t]
    even = core == 0

    def choose(a, c):
        return jnp.where(even, a.astype(jnp.float32), c.astype(jnp.float32)).astype(jnp.bfloat16)

    t_cat = jnp.concatenate(
        [
            choose(pair_t[2], pair_t[1]),
            choose(pair_t[1], pair_t[2]),
            choose(pair_t[0], pair_t[3]),
            choose(pair_t[3], pair_t[0]),
        ],
        axis=0,
    )
    def turn_rows(k, carry):
        rows = pl.ds(pl.multiple_of(k * 512, 512), 512)
        left = jnp.concatenate([fbuf[s, rows, :] for s in (1, 2, 3, 4)], axis=1)
        d = dot(left, t_cat)
        right_ref[rows, :] = d[:, 0:128] + d[:, 128:256]
        return carry

    for k in (0, 1):

        @pl.when(tau < 0)
        def _():
            factor_copy(1, k).wait_recv()

        @pl.when(tau > 0)
        def _():
            factor_copy(0, k).wait_recv()

        far_copy(k).wait_recv()
        steps = depth // 1024
        lax.fori_loop(k * steps, (k + 1) * steps, turn_rows, 0)

    for copy in pending:
        copy.wait_send()
    for ahead, copy in groups:

        @pl.when(ahead != 0)
        def _():
            copy.wait_send()


def per_device(weight, factor, pairing):
    rows, depth = weight.shape
    vmem = pl.BlockSpec(memory_space=pltpu.VMEM)
    f32, b16 = jnp.float32, jnp.bfloat16
    dma = pltpu.SemaphoreType.DMA
    n_gram = len(GRAM)
    rotated, right = pl.pallas_call(
        kernel,
        out_shape=(jax.ShapeDtypeStruct((8, 2, 2, 8, 128), f32), jax.ShapeDtypeStruct((depth, 128), f32)),
        in_specs=[pl.BlockSpec(memory_space=pltpu.HBM)] * 3,
        out_specs=(vmem, vmem),
        scratch_shapes=[
            pltpu.VMEM((rows, depth), b16),
            pltpu.VMEM(pairing.shape, jnp.int32),
            pltpu.VMEM((NX * NZ * HALF, 2 * rows, depth // 2), b16),
            pltpu.VMEM((6, depth, 128), b16),
            pltpu.VMEM((NX * NZ, HALF * rows, 256), f32),
            pltpu.VMEM((3, NZ, HALF * rows, 256), f32),
            pltpu.VMEM((NX, NZ * HALF * rows, 256), f32),
            pltpu.VMEM((3, NZ * HALF * rows, 256), f32),
            pltpu.VMEM((4, 64, 128), f32),
            pltpu.VMEM((4, 2, 2, 64, 128), f32),
            pltpu.VMEM((8, 256, 256), f32),
            pltpu.VMEM((n_gram, 128), f32),
            pltpu.VMEM((4, n_gram, 128), f32),
            pltpu.VMEM((8, 128, 256), b16),
            pltpu.VMEM((8, 128, 128), f32),
            pltpu.VMEM((16, 128), f32),
            dma((len(TREE),)),
            dma((len(TREE),)),
            dma,
            dma,
            dma,
            dma((9,)),
            dma((9,)),
            dma((NX * NZ,)),
            dma((3, NZ)),
            dma((NX,)),
            dma((3,)),
            dma((4, 4)),
            dma((4, 2, 2)),
            dma((3,)),
            dma((4,)),
        ],
        compiler_params=pltpu.CompilerParams(
            collective_id=0, has_side_effects=True, vmem_limit_bytes=60 * 2**20
        ),
        name="whiten_turn",
    )(weight, factor, pairing)
    return rotated.reshape(256, 128), right


def solution(mesh):
    in_specs = (P("blk", "rows"), P("rows", "blk"), P())
    out_specs = (P("rows", "blk"), P("rows", "blk"))
    return jax.shard_map(per_device, mesh=mesh, in_specs=in_specs, out_specs=out_specs, check_vma=False)
```
